32 devices in a mesh: groups: 2 (over x), ctx: 8 (over z, y), fsdp: 2 (over core).
Axes of the slice: x: 2, y: 2, z: 4, core: 2. Of those that a mesh axis runs over, the one named last changes fastest.
Arguments:
- tokens: bfloat16 [4096, 4096], P(('groups', 'ctx', 'fsdp')), parts along dimension 0, may hold values from -6 to 6
- routed_index: int32 [32, 24], P(('groups', 'ctx', 'fsdp')), parts along dimension 0, may hold values from 0 to 127, as said below
- routed_count: int32 [32], P(('groups', 'ctx', 'fsdp')), parts along dimension 0, may hold values from 1 to 24, 256 in all
- router_weight: float32 [4096], replicated, may hold values from -0.09375 to 0.09375
- attn_gain: float32 [4096], replicated, may hold values from 0.5 to 2
- ffn_gain: float32 [4096], replicated, may hold values from 0.5 to 2
- w_query: bfloat16 [4096, 2048], P(None, ('ctx', 'fsdp'))
- w_keyvalue: bfloat16 [4096, 1024], P('fsdp', 'ctx')
- w_out: bfloat16 [2048, 4096], P(('ctx', 'fsdp')), may hold values from -0.125 to 0.125
- w_gate: bfloat16 [4096, 7168], P('fsdp', 'ctx'), may hold values from -0.09375 to 0.09375
- w_up: bfloat16 [4096, 7168], P('fsdp', 'ctx'), may hold values from -0.09375 to 0.09375
- w_down: bfloat16 [7168, 4096], P('ctx', 'fsdp'), may hold values from -0.0625 to 0.0625
Outputs:
- blended: bfloat16 [4096, 4096], P(('groups', 'ctx', 'fsdp')), parts along dimension 0
The draws below stay inside these ranges and needn't reach their ends.
There are 2 independent parts, one for each index of `groups`. The reference program is written for one: setup_inputs(seed, part) draws one part's arguments, and reference() takes and returns one part's arrays. A program takes and returns all parts, laid end to end along the dimension named above; an argument that names none is the same for every part. Nothing has to cross between parts.
Inputs may be any that keep to these rules, and one draw needn't show every extreme that they name: `routed_index`: row s holds 24 different rows of the s-th block of 128 tokens in increasing order; its first routed_count[s] entries are the routed ones. `routed_count`: the counts add up to 256.
All inputs are finite; a program needn't handle non-finite values. No bound on the sum of `routed_count` on one device may be relied on, other than what follows from the above.
Results may differ from the reference program's by a relative error of at most 0.0035.
Values may be sent and summed in bfloat16 or wider, within the bound.
A program may use at most 128 MiB of HBM per device.

```python
import math
import jax
import jax.numpy as jnp
import numpy as np
from jax import lax

D = 4096
HD = 128
TOK_DEV = 128
SHARDS = 16
HEADS = 16
KV_HEADS = 4
FF = 7168
CAP = 24
TOKENS = 2048
ROUTED = 256


def draw_w_query(key, part):
    key = jax.random.fold_in(key, 1)
    own = jnp.clip(jax.random.normal(key, (D, HEADS, HD), jnp.float32), -5.0, 5.0)
    return (own / math.sqrt(D)).reshape(D, HEADS * HD).astype(jnp.bfloat16)


def draw_w_keyvalue(key, part):
    key = jax.random.fold_in(key, 2)
    own = jnp.clip(jax.random.normal(key, (D, HEADS // 4, 2, HD), jnp.float32), -5.0, 5.0)
    return (own / math.sqrt(D)).reshape(D, HEADS // 4 * 2 * HD).astype(jnp.bfloat16)


def draw_routed_index(key, part):
    key = jax.random.fold_in(key, 3)
    keys = jax.random.split(key, SHARDS)

    def one_shard(shard_key):
        return jnp.sort(jax.random.permutation(shard_key, TOK_DEV)[:CAP])
    return jax.vmap(one_shard)(keys).astype(jnp.int32)


def steps_of(key, dims, cuts, least, largest):
    def one(axis_at, blocks):
        steps = jax.random.uniform(jax.random.fold_in(jax.random.fold_in(key, 6), axis_at), (blocks,), jnp.float32, least / len(cuts), largest / len(cuts))
        return jnp.repeat(jnp.exp(steps), dims[axis_at] // blocks).reshape((-1,) + (1,) * (len(dims) - axis_at - 1))

    level = one(*cuts[0])
    for cut in cuts[1:]:
        level = level * one(*cut)
    return level


def split_up(count, total, most, slope):
    portions = [(1 << 20) // math.isqrt(standing ** slope) + 1 for standing in range(2, count + 1)]
    surplus, given = total - most - (count - 1), [1] * (count - 1)
    while surplus > 0:
        free = [i for i in range(count - 1) if given[i] < most]
        pool, remaining = sum([portions[i] for i in free]), surplus
        for i in free:
            more = min(most - given[i], max(1, remaining * portions[i] // pool), surplus)
            given[i] = given[i] + more
            surplus = surplus - more
    return np.array([most] + given)


def uneven(key, number_of, total, reach, lean):
    if number_of == 2:
        one = jax.random.randint(key, (), max(1, total - reach), min(reach, total - 1) + 1)
        return jnp.stack([one, total - one])
    tallies = jnp.asarray(split_up(number_of, total, reach, lean), jnp.int32)
    couples = (number_of - 1) // 2
    source_of, receiver = tallies[1:1 + 2 * couples:2], tallies[2:2 + 2 * couples:2]
    slack = jnp.minimum(source_of - 1, reach - receiver)
    moved = jax.random.randint(jax.random.fold_in(key, 1), (couples,), 0, 1 << 20) % (slack + 1)
    tallies = tallies.at[1:1 + 2 * couples:2].set(source_of - moved).at[2:2 + 2 * couples:2].set(receiver + moved)
    return tallies[jax.random.permutation(jax.random.fold_in(key, 2), number_of)]


def bell_draw(own_key, extent, deviation, limit, cuts=(), kind=jnp.bfloat16):
    drawn = deviation * jax.random.normal(own_key, extent, jnp.float32)
    if cuts:
        drawn = drawn * steps_of(own_key, extent, cuts, -0.22, 0.18)
    return jnp.clip(drawn, -limit, limit).astype(kind)


def setup_inputs(seed: int = 0, part: int = 0) -> dict:
    streams_of = jax.random.split(jax.random.key(seed), 13)
    part_keys = jax.random.split(jax.random.fold_in(streams_of[12], part), 13)
    tokens = bell_draw(part_keys[0], (TOKENS, D), 1.0, 6.0, ((0, 16),))
    routed_index = draw_routed_index(jax.random.fold_in(jax.random.fold_in(streams_of[12], part), 71), part)
    routed_count = uneven(part_keys[2], SHARDS, ROUTED, CAP, 2).astype(jnp.int32)
    router_weight = bell_draw(streams_of[3], (D,), D ** -0.5, 0.09375, (), jnp.float32)
    attn_gain = jnp.clip(jnp.exp(jax.random.uniform(streams_of[4], (D,), jnp.float32, math.log(0.5), math.log(2.0))), 0.5, 2.0)
    ffn_gain = jnp.clip(jnp.exp(jax.random.uniform(streams_of[5], (D,), jnp.float32, math.log(0.5), math.log(2.0))), 0.5, 2.0)
    w_query = draw_w_query(jax.random.fold_in(streams_of[12], 71), part)
    w_keyvalue = draw_w_keyvalue(jax.random.fold_in(streams_of[12], 71), part)
    w_out = bell_draw(streams_of[8], (HEADS * HD, D), (HEADS * HD) ** -0.5, 0.125, ((0, 16),))
    w_gate = bell_draw(streams_of[9], (D, FF), D ** -0.5, 0.09375, ((0, 2), (1, 8)))
    w_up = bell_draw(streams_of[10], (D, FF), D ** -0.5, 0.09375, ((0, 2), (1, 8)))
    w_down = bell_draw(streams_of[11], (FF, D), FF ** -0.5, 0.0625, ((0, 8), (1, 2)))
    return dict(tokens=tokens, routed_index=routed_index, routed_count=routed_count, router_weight=router_weight, attn_gain=attn_gain, ffn_gain=ffn_gain, w_query=w_query, w_keyvalue=w_keyvalue, w_out=w_out, w_gate=w_gate, w_up=w_up, w_down=w_down)


def rms_norm(values, gain):
    scale = lax.rsqrt(lax.optimization_barrier(jnp.mean(values * values, axis=-1, keepdims=True)) + 1e-05)
    return (values * scale * gain).astype(jnp.bfloat16)

def rotate(block, position):
    width = block.shape[-1]
    half = width // 2
    freq = jnp.exp(-math.log(500000.0) * jnp.arange(half, dtype=jnp.float32) * 2.0 / width)
    angle = position.astype(jnp.float32)[:, None, None] * freq[None, None, :]
    cosine = jnp.cos(angle)
    sine = jnp.sin(angle)
    first = block[..., :half]
    second = block[..., half:]
    return jnp.concatenate([first * cosine - second * sine, second * cosine + first * sine], axis=-1)

def reference(tokens, routed_index, routed_count, router_weight, attn_gain, ffn_gain, w_query, w_keyvalue, w_out, w_gate, w_up, w_down):
    shards, slots = routed_index.shape
    tok_rows = tokens.shape[0] // shards
    count = shards * slots
    position = (jnp.arange(shards, dtype=jnp.int32)[:, None] * tok_rows + routed_index.astype(jnp.int32)).reshape(-1)
    live = (jnp.arange(slots, dtype=jnp.int32)[None, :] < routed_count[:, None]).reshape(-1)
    picked = tokens[position]
    base = picked.astype(jnp.float32)
    normed = rms_norm(base, attn_gain)
    query = jnp.dot(normed, w_query, preferred_element_type=jnp.float32).reshape(count, HEADS, HD)
    query = rotate(query, position).astype(jnp.bfloat16)
    pairs = jnp.dot(normed, w_keyvalue, preferred_element_type=jnp.float32).reshape(count, KV_HEADS, 2, HD)
    keys = rotate(pairs[:, :, 0], position).astype(jnp.bfloat16)
    values = pairs[:, :, 1].astype(jnp.bfloat16)
    allowed = live[None, :] & (position[None, :] <= position[:, None])
    scale = 1.0 / math.sqrt(HD)
    q_groups = query.reshape(count, KV_HEADS, 4, HD).transpose(1, 2, 0, 3)
    k_groups = keys.transpose(1, 0, 2)
    v_groups = values.transpose(1, 0, 2)

    def group(operands):
        q_part, k_part, v_part = operands
        scores = jnp.einsum('hqd,kd->hqk', q_part.astype(jnp.float32), k_part.astype(jnp.float32)) * scale
        scores = jnp.where(allowed[None], scores, -1e+30)
        top = lax.optimization_barrier(jnp.max(scores, axis=-1, keepdims=True))
        weights = jnp.exp(scores - top)
        probs = (weights / lax.optimization_barrier(jnp.sum(weights, axis=-1, keepdims=True))).astype(jnp.bfloat16)
        return jnp.einsum('hqk,kd->hqd', probs.astype(jnp.float32), v_part.astype(jnp.float32)).astype(jnp.bfloat16)
    mixed = lax.map(group, (q_groups, k_groups, v_groups))
    mixed = mixed.transpose(2, 0, 1, 3).reshape(count, HEADS * HD)
    attention = jnp.dot(mixed, w_out, preferred_element_type=jnp.float32)
    resid = base + attention
    normed_two = rms_norm(resid, ffn_gain)
    gate_part = jnp.dot(normed_two, w_gate, preferred_element_type=jnp.float32)
    up_part = jnp.dot(normed_two, w_up, preferred_element_type=jnp.float32)
    hidden = (jax.nn.silu(gate_part) * up_part).astype(jnp.bfloat16)
    feed = jnp.dot(hidden, w_down, preferred_element_type=jnp.float32)
    router = jax.nn.sigmoid(jnp.dot(base, router_weight, precision=lax.Precision.HIGHEST))
    updated = (base + router[:, None] * (attention + feed)).astype(jnp.bfloat16)
    target = jnp.where(live, position, tokens.shape[0]).astype(jnp.int32)
    return tokens.at[target].set(updated, mode='drop')
```

```python
import functools
import math

import jax
import jax.numpy as jnp
from jax import lax
from jax.experimental import pallas as pl
from jax.experimental.pallas import tpu as pltpu
from jax.sharding import PartitionSpec as P

F32 = jnp.float32
BF16 = jnp.bfloat16
MESH = pl.DeviceIdType.MESH
CAP = 24
BLK = 48
ROW = 32
META = 128
CHUNK = 512


def dot(a, b):
    return jnp.dot(a, b, preferred_element_type=F32)


def rope(u, cosine, sine):
    return u * cosine + pltpu.roll(u, 64, 1) * sine


def kernel(
    m, d, tok_rows,
    x_ref, again_ref, fgain_ref, wq_hbm, wkv_hbm, wo_hbm, wg_hbm, wu_hbm, wd_hbm,
    out_ref,
    grid, wq, wkv, wo, wg, wu, wd,
    meta, picked, normed, kvp, kvp_in, kv, kv_in, mix,
    pb, rb, sb, tb, att, ssq, n2, gu, gu_in, hid, pc, pd, rd, sd, td, dl, dr,
    lsem, ssem, rsem,
):
    half = d // 2
    shards = 4 * m
    rows = 16 * shards
    nch = half // CHUNK
    c = lax.axis_index("ctx")
    f = lax.axis_index("fsdp")
    hi, lo = c // 2, lax.rem(c, 2)
    sib = {"fsdp": 1 - f}
    pair = {"ctx": hi * 2 + 1 - lo}

    def across(k):
        return {"ctx": lax.rem(hi + k, m) * 2 + lo}

    def source(k):
        return lax.rem(hi + m - k, m)

    taken = [0]
    sent = []

    def remote(src, dst, to):
        i = taken[0]
        taken[0] += 1
        copy = pltpu.make_async_remote_copy(
            src_ref=src, dst_ref=dst, send_sem=ssem.at[i], recv_sem=rsem.at[i],
            device_id=to, device_id_type=MESH,
        )
        copy.start()
        sent.append(copy)
        return copy

    barrier = pltpu.get_barrier_semaphore()
    for to in [sib, pair] + [across(k) for k in range(1, m)]:
        pl.semaphore_signal(barrier, inc=1, device_id=to, device_id_type=MESH)
    pl.semaphore_wait(barrier, m + 1)

    def gather(block, dest, with_sib):
        ahead = [remote(block, dest(lo, hi), across(k)) for k in range(1, m)]
        by_pair = [remote(block, dest(lo, hi), pair)]
        by_sib = []
        if with_sib:
            by_sib.append(remote(block, dest(lo, hi), sib))
        for k in range(1, m):
            ahead[k - 1].wait_recv()
            at = dest(lo, source(k))
            by_pair.append(remote(at, at, pair))
            if with_sib:
                by_sib.append(remote(at, at, sib))
        for k in range(m):
            by_pair[k].wait_recv()
            if with_sib:
                at = dest(1 - lo, source(k) if k else hi)
                by_sib.append(remote(at, at, sib))
        for copy in by_sib:
            copy.wait_recv()

    loads = []

    def load(src, dst):
        copy = pltpu.make_async_copy(src, dst, lsem.at[len(loads)])
        copy.start()
        loads.append(copy)
        return copy

    mine = pl.ds(pl.multiple_of(f * half, 128), half)
    other = pl.ds(pl.multiple_of((1 - f) * half, 128), half)
    get_wq, get_wkv = load(wq_hbm, wq), load(wkv_hbm, wkv)
    get_wo = load(wo_hbm.at[:, mine], wo.at[f])
    get_wg, get_wu, get_wd = load(wg_hbm, wg), load(wu_hbm, wu), load(wd_hbm, wd)
    grid[lo, hi, f] = x_ref[...]
    gather(x_ref, lambda a, b: grid.at[a, b, f], True)
    wo_in = remote(wo_hbm.at[:, other], wo.at[f], sib)

    total = shards * BLK
    for a in range(2):
        for b in range(m):
            for e in range(2):
                at = ((a * m + b) * 2 + e) * CAP
                meta[at:at + CAP] = grid[a, b, e, :, half:].astype(F32)[:CAP]

    def shard_of(block):
        return lax.rem(block // 2, m) * 4 + block // (2 * m) * 2 + lax.rem(block, 2)

    lanes = grid[:, :, :, :, half:].reshape(total, META).astype(F32).T
    glane = lax.broadcasted_iota(jnp.int32, (8, total), 1)
    gslot = lax.rem(glane, BLK)
    count_l = jnp.broadcast_to(lanes[1:2], (8, total))
    first = jnp.where(gslot == 0, count_l, 0.0).astype(BF16)
    tri = shard_of(lax.broadcasted_iota(jnp.int32, (total, total), 0) // BLK) < shard_of(
        lax.broadcasted_iota(jnp.int32, (total, total), 1) // BLK)
    start_l = dot(first, tri.astype(F32).astype(BF16))
    wide = gslot.astype(F32)
    left = jnp.where(wide < count_l, start_l + wide, -1.0)[:1]
    wide = wide - CAP
    right = jnp.where((wide >= 0) & (wide < count_l), start_l + wide, -1.0)[:1]
    place = lax.broadcasted_iota(jnp.int32, (rows, total), 0).astype(F32)
    left = jnp.where(left == place, 1.0, 0.0).astype(BF16)
    right = jnp.where(right == place, 1.0, 0.0).astype(BF16)

    square = jnp.zeros((rows, 1), F32)
    for h, pick in enumerate((left, right)):
        for j in range(nch):
            cut = slice(j * CHUNK, (j + 1) * CHUNK)
            got = dot(pick, grid[:, :, :, :, cut].reshape(total, CHUNK))
            square = square + jnp.sum(got * got, axis=1, keepdims=True)
            picked[h, :, cut] = got.astype(BF16)
    scale = lax.rsqrt(square / d + 1e-05)
    for h in range(2):
        for j in range(nch):
            cut = slice(j * CHUNK, (j + 1) * CHUNK)
            normed[h, :, cut] = (
                picked[h, :, cut].astype(F32) * scale * again_ref[h, :, cut]).astype(BF16)

    get_wkv.wait()
    kvp[...] = dot(normed[f], wkv[...])
    kvp_in_copy = remote(kvp, kvp_in, sib)
    info = dot(left, grid[:, :, :, :, half:].reshape(total, META))
    position = info[:, 2:3] * tok_rows + info[:, 0:1]
    lane = lax.broadcasted_iota(jnp.int32, (rows, 128), 1)
    freq = jnp.exp(-math.log(500000.0) * lax.rem(lane, 64).astype(F32) * 2.0 / 128)
    angle = position * freq
    cosine = jnp.cos(angle)
    sine = jnp.where(lane < 64, -1.0, 1.0) * jnp.sin(angle)
    get_wq.wait()
    query = rope(dot(normed[0], wq[:half]) + dot(normed[1], wq[half:]), cosine, sine).astype(BF16)
    kvp_in_copy.wait_recv()
    both = kvp[...] + kvp_in[...]
    holds_keys = lo == 0
    kv[...] = jnp.where(holds_keys, rope(both, cosine, sine), both).astype(BF16)
    kv_copy = remote(kv, kv_in, pair)
    kv_copy.wait_recv()
    keys = jnp.where(holds_keys, kv[...].astype(F32), kv_in[...].astype(F32)).astype(BF16)
    values = jnp.where(holds_keys, kv_in[...].astype(F32), kv[...].astype(F32)).astype(BF16)
    scores = lax.dot_general(query, keys, (((1,), (1,)), ((), ())), preferred_element_type=F32)
    scores = scores * (1.0 / math.sqrt(128))
    seen = lax.broadcasted_iota(jnp.int32, (rows, rows), 1) <= lax.broadcasted_iota(
        jnp.int32, (rows, rows), 0)
    scores = jnp.where(seen, scores, -1e30)
    weights = jnp.exp(scores - jnp.max(scores, axis=1, keepdims=True))
    probs = (weights / jnp.sum(weights, axis=1, keepdims=True)).astype(BF16)
    mix[f] = dot(probs, values).astype(BF16)
    mix_copy = remote(mix.at[f], mix.at[f], sib)
    get_wo.wait()
    wo_in.wait_recv()
    mix_copy.wait_recv()

    def scatter(part, order, size, pbuf, rbuf, sbuf, tbuf, take):
        passed = []
        for j in range(nch):
            value = part(j)
            for a in range(2):
                for b in range(m):
                    at = order(a, b) * size
                    pbuf[j, a, b] = value[at:at + size].astype(BF16)
            passed.append(remote(pbuf.at[j, 1 - lo], rbuf.at[j], pair))
        spread = []
        for j in range(nch):
            passed[j].wait_recv()
            sbuf[j] = (pbuf[j, lo].astype(F32) + rbuf[j].astype(F32)).astype(BF16)
            spread.append([
                remote(sbuf.at[j, lax.rem(hi + k, m)], tbuf.at[j, k - 1], across(k))
                for k in range(1, m)])
        for j in range(nch):
            whole = pbuf[j, lo, hi].astype(F32) + rbuf[j, hi].astype(F32)
            for k in range(1, m):
                spread[j][k - 1].wait_recv()
                whole = whole + tbuf[j, k - 1].astype(F32)
            take(j, whole)

    mixed = jnp.concatenate([mix[0], mix[1]], axis=1)

    def project(j):
        cut = slice(j * CHUNK, (j + 1) * CHUNK)
        return dot(mixed, wo[:, :, cut].reshape(256, CHUNK))

    own = pl.ds(pl.multiple_of(c * ROW, ROW), ROW)

    def keep(j, whole):
        att[:, j * CHUNK:(j + 1) * CHUNK] = whole

    scatter(project, lambda a, b: b * 2 + a, ROW, pb, rb, sb, tb, keep)

    resid = picked[f, own, :].astype(F32) + att[...]
    ssq[0] = jnp.broadcast_to(jnp.sum(resid * resid, axis=1, keepdims=True), (ROW, 128))
    remote(ssq.at[0], ssq.at[1], sib).wait_recv()
    scale2 = lax.rsqrt((ssq[0] + ssq[1])[:, :1] / d + 1e-05)
    n2[lo, hi] = (resid * scale2 * fgain_ref[f]).astype(BF16)
    gather(n2.at[lo, hi], lambda a, b: n2.at[a, b], False)

    get_wg.wait()
    get_wu.wait()
    ff = wg.shape[1]
    hrows = rows // 2
    away = n2[1 - f].reshape(hrows, half)
    gu[0] = dot(away, wg[...]).astype(BF16)
    gu[1] = dot(away, wu[...]).astype(BF16)
    gu_copy = remote(gu, gu_in, sib)
    home = n2[f].reshape(hrows, half)
    gate = dot(home, wg[...])
    up = dot(home, wu[...])
    gu_copy.wait_recv()
    gate = gate + gu_in[0].astype(F32)
    up = up + gu_in[1].astype(F32)
    hid[f] = (gate / (1.0 + jnp.exp(-gate)) * up).astype(BF16)
    hid_copy = remote(hid.at[f], hid.at[f], sib)

    slots = shards * CAP
    sub = lax.broadcasted_iota(jnp.int32, (slots, META), 0)
    count_s = meta[:, 1:2]
    lead = jnp.where(lax.rem(sub, CAP) == 0, meta[...], 0.0).astype(BF16)
    tri_s = shard_of(lax.broadcasted_iota(jnp.int32, (slots, slots), 1) // CAP) < shard_of(
        lax.broadcasted_iota(jnp.int32, (slots, slots), 0) // CAP)
    start_s = dot(tri_s.astype(F32).astype(BF16), lead)[:, 1:2]
    slot_s = lax.rem(sub, CAP)[:, :1].astype(F32)
    target = jnp.where(slot_s < count_s, start_s + slot_s, -1.0)
    p = lax.broadcasted_iota(jnp.int32, (slots, rows), 1)
    natural = (lax.rem(p // ROW, m) * 2 + p // (ROW * m)) * ROW + lax.rem(p, ROW)
    expand = jnp.where(target == natural.astype(F32), 1.0, 0.0).astype(BF16)

    get_wd.wait()
    hid_copy.wait_recv()
    hidden = hid[...].reshape(rows, ff)
    own_perm = pl.ds(pl.multiple_of((lo * m + hi) * ROW, ROW), ROW)

    def feed(j):
        cut = slice(j * CHUNK, (j + 1) * CHUNK)
        pc[...] = dot(hidden, wd[:, cut])
        pc[own_perm, :] += att[:, cut]
        return dot(expand, pc[...].astype(BF16))

    def deliver(j, whole):
        cut = slice(j * CHUNK, (j + 1) * CHUNK)
        dl[0, :, cut] = whole[:CAP]
        dl[1, :, cut] = whole[CAP:]

    scatter(feed, lambda a, b: a * m + b, BLK, pd, rd, sd, td, deliver)
    remote(dl.at[1 - f], dr, sib).wait_recv()
    out_ref[f] = dl[f]
    out_ref[1 - f] = dr[...]
    for copy in sent:
        copy.wait_send()


def body(
    tokens, routed_index, routed_count, router_weight, attn_gain, ffn_gain,
    w_query, w_keyvalue, w_out, w_gate, w_up, w_down,
):
    tok_rows, d = tokens.shape
    half = d // 2
    n = lax.axis_size("ctx")
    m = n // 2
    shards = 2 * n
    rows = 16 * shards
    slots = shards * CAP
    nch = half // CHUNK
    ff = w_gate.shape[1]
    index_row = routed_index[0]
    picked = jnp.take(tokens, index_row, axis=0)
    shard = lax.axis_index("ctx") * 2 + lax.axis_index("fsdp")
    lane = jnp.arange(META)[None, :]
    facts = jnp.where(
        lane == 0, index_row[:, None],
        jnp.where(lane == 1, routed_count[0], jnp.where(lane == 2, shard, 0))).astype(BF16)
    block = jnp.concatenate(
        [jnp.concatenate([picked[:, :half], facts], 1),
         jnp.concatenate([picked[:, half:], facts], 1)], 0)
    copies = 4 * m - 1 + 4 + 2 * nch * m + 1 + 2 * m - 1 + 3 + 8
    vm = pl.BlockSpec(memory_space=pltpu.VMEM)
    hbm = pl.BlockSpec(memory_space=pl.ANY)
    flops = 2 * rows * half * ff * 3
    delta = pl.pallas_call(
        functools.partial(kernel, m, d, tok_rows),
        out_shape=jax.ShapeDtypeStruct((2, CAP, half), F32),
        in_specs=[vm] * 3 + [hbm] * 6,
        out_specs=vm,
        scratch_shapes=[
            pltpu.VMEM((2, m, 2, BLK, half + META), BF16),
            pltpu.VMEM(w_query.shape, BF16),
            pltpu.VMEM(w_keyvalue.shape, BF16),
            pltpu.VMEM((2, 128, half), BF16),
            pltpu.VMEM(w_gate.shape, BF16),
            pltpu.VMEM(w_up.shape, BF16),
            pltpu.VMEM(w_down.shape, BF16),
            pltpu.VMEM((slots, META), F32),
            pltpu.VMEM((2, rows, half), BF16),
            pltpu.VMEM((2, rows, half), BF16),
            pltpu.VMEM((rows, 128), F32),
            pltpu.VMEM((rows, 128), F32),
            pltpu.VMEM((rows, 128), BF16),
            pltpu.VMEM((rows, 128), BF16),
            pltpu.VMEM((2, rows, 128), BF16),
            pltpu.VMEM((nch, 2, m, ROW, CHUNK), BF16),
            pltpu.VMEM((nch, m, ROW, CHUNK), BF16),
            pltpu.VMEM((nch, m, ROW, CHUNK), BF16),
            pltpu.VMEM((nch, m - 1, ROW, CHUNK), BF16),
            pltpu.VMEM((ROW, half), F32),
            pltpu.VMEM((2, ROW, 128), F32),
            pltpu.VMEM((2, m, ROW, half), BF16),
            pltpu.VMEM((2, rows // 2, ff), BF16),
            pltpu.VMEM((2, rows // 2, ff), BF16),
            pltpu.VMEM((2, rows // 2, ff), BF16),
            pltpu.VMEM((rows, CHUNK), F32),
            pltpu.VMEM((nch, 2, m, BLK, CHUNK), BF16),
            pltpu.VMEM((nch, m, BLK, CHUNK), BF16),
            pltpu.VMEM((nch, m, BLK, CHUNK), BF16),
            pltpu.VMEM((nch, m - 1, BLK, CHUNK), BF16),
            pltpu.VMEM((2, CAP, half), F32),
            pltpu.VMEM((CAP, half), F32),
            pltpu.SemaphoreType.DMA((6,)),
            pltpu.SemaphoreType.DMA((copies,)),
            pltpu.SemaphoreType.DMA((copies,)),
        ],
        compiler_params=pltpu.CompilerParams(
            collective_id=0, has_side_effects=True, vmem_limit_bytes=60 * 1024 * 1024),
        cost_estimate=pl.CostEstimate(flops=flops, bytes_accessed=14 << 20, transcendentals=0),
        name="depth_block",
    )(block, attn_gain.reshape(2, 1, half), ffn_gain.reshape(2, 1, half),
      w_query, w_keyvalue, w_out, w_gate, w_up, w_down)
    base = picked.astype(F32)
    router = jax.nn.sigmoid(jnp.dot(base, router_weight, precision=lax.Precision.HIGHEST))
    delta = jnp.concatenate([delta[0], delta[1]], axis=1)
    updated = (base + router[:, None] * delta).astype(BF16)
    live = jnp.arange(CAP, dtype=jnp.int32) < routed_count[0]
    hit = (jnp.arange(tok_rows, dtype=jnp.int32)[:, None] == index_row[None, :]) & live[None, :]
    placed = jnp.dot(hit.astype(BF16), updated, preferred_element_type=F32).astype(BF16)
    return jnp.where(jnp.any(hit, axis=1)[:, None], placed, tokens)


def solution(mesh):
    placed = (
        P(("groups", "ctx", "fsdp"), None),
        P(("groups", "ctx", "fsdp"), None),
        P(("groups", "ctx", "fsdp")),
        P(),
        P(),
        P(),
        P(None, ("ctx", "fsdp")),
        P("fsdp", "ctx"),
        P(("ctx", "fsdp"), None),
        P("fsdp", "ctx"),
        P("fsdp", "ctx"),
        P("ctx", "fsdp"),
    )
    return jax.shard_map(
        body,
        mesh=mesh,
        in_specs=placed,
        out_specs=P(("groups", "ctx", "fsdp"), None),
        check_vma=False,
    )
```

```python
import functools
import math

import jax
import jax.numpy as jnp
from jax import lax
from jax.experimental import pallas as pl
from jax.experimental.pallas import tpu as pltpu
from jax.sharding import PartitionSpec as P

F32 = jnp.float32
BF16 = jnp.bfloat16
MESH = pl.DeviceIdType.MESH
CAP = 24
BLK = 48
ROW = 32
META = 128
CHUNK = 512
SUM = 256
PIECES = 4


def dot(a, b):
    return jnp.dot(a, b, preferred_element_type=F32)


def rope(u, cosine, sine):
    return u * cosine + pltpu.roll(u, 64, 1) * sine


def kernel(
    m, d, tok_rows,
    x_ref, again_ref, fgain_ref, wq_hbm, wkv_hbm, wo_hbm, wg_hbm, wu_hbm, wd_hbm,
    out_ref,
    grid, wq, wkv, wo, wg, wu, wd,
    meta, picked, normed, kvp, kvp_in, kv, kv_in, mix,
    pb, rb, sb, tb, att, ssq, n2, gu, gu_in, hid, pc, pd, rd, sd, td, dl, dr,
    lsem, ssem, rsem,
):
    half = d // 2
    shards = 4 * m
    rows = 16 * shards
    nch = half // CHUNK
    c = lax.axis_index("ctx")
    f = lax.axis_index("fsdp")
    hi, lo = c // 2, lax.rem(c, 2)
    sib = {"fsdp": 1 - f}
    pair = {"ctx": hi * 2 + 1 - lo}

    def across(k):
        return {"ctx": lax.rem(hi + k, m) * 2 + lo}

    def source(k):
        return lax.rem(hi + m - k, m)

    taken = [0]
    sent = []

    def remote(src, dst, to):
        i = taken[0]
        taken[0] += 1
        copy = pltpu.make_async_remote_copy(
            src_ref=src, dst_ref=dst, send_sem=ssem.at[i], recv_sem=rsem.at[i],
            device_id=to, device_id_type=MESH,
        )
        copy.start()
        sent.append(copy)
        return copy

    barrier = pltpu.get_barrier_semaphore()
    for to in [sib, pair] + [across(k) for k in range(1, m)]:
        pl.semaphore_signal(barrier, inc=1, device_id=to, device_id_type=MESH)
    pl.semaphore_wait(barrier, m + 1)

    def gather(block, dest, width, with_sib, between):
        size = half // PIECES
        cuts = [pl.ds(p * size, size if p < PIECES - 1 else width - p * size)
                for p in range(PIECES)]
        ahead, by_pair, by_sib = [], [], []
        for cut in cuts:
            near = dest(lo, hi).at[:, cut]
            ahead.append([remote(block.at[:, cut], near, across(k)) for k in range(1, m)])
            by_pair.append([remote(block.at[:, cut], near, pair)])
            if with_sib:
                by_sib.append(remote(block.at[:, cut], near, sib))
        between()
        for p, cut in enumerate(cuts):
            for k in range(1, m):
                ahead[p][k - 1].wait_recv()
                at = dest(lo, source(k)).at[:, cut]
                by_pair[p].append(remote(at, at, pair))
                if with_sib:
                    by_sib.append(remote(at, at, sib))
            if p:
                drain(p - 1, cuts[p - 1], dest, by_pair, by_sib, with_sib)
        drain(PIECES - 1, cuts[-1], dest, by_pair, by_sib, with_sib)
        for copy in by_sib:
            copy.wait_recv()

    def drain(p, cut, dest, by_pair, by_sib, with_sib):
        for k in range(m):
            by_pair[p][k].wait_recv()
            if with_sib:
                at = dest(1 - lo, source(k) if k else hi).at[:, cut]
                by_sib.append(remote(at, at, sib))

    loads = []

    def load(src, dst):
        copy = pltpu.make_async_copy(src, dst, lsem.at[len(loads)])
        copy.start()
        loads.append(copy)
        return copy

    mine = pl.ds(pl.multiple_of(f * half, 128), half)
    other = pl.ds(pl.multiple_of((1 - f) * half, 128), half)
    get_wq, get_wkv = load(wq_hbm, wq), load(wkv_hbm, wkv)
    get_wo = load(wo_hbm.at[:, mine], wo.at[f])
    get_wg, get_wu, get_wd = load(wg_hbm, wg), load(wu_hbm, wu), load(wd_hbm, wd)
    grid[lo, hi, f] = x_ref[...]
    total = shards * BLK
    slots = shards * CAP
    held = []

    def shard_of(block):
        return lax.rem(block // 2, m) * 4 + block // (2 * m) * 2 + lax.rem(block, 2)

    def tables():
        down = shard_of(lax.broadcasted_iota(jnp.int32, (total, 1), 0) // BLK)
        along = shard_of(lax.broadcasted_iota(jnp.int32, (1, total), 1) // BLK)
        held.append((down < along).astype(F32).astype(BF16))

    gather(x_ref, lambda a, b: grid.at[a, b, f], half + META, True, tables)
    wo_in = remote(wo_hbm.at[:, other], wo.at[f], sib)

    for a in range(2):
        for b in range(m):
            for e in range(2):
                at = ((a * m + b) * 2 + e) * CAP
                meta[at:at + CAP] = grid[a, b, e, :, half:].astype(F32)[:CAP]

    lanes = grid[:, :, :, :, half:].reshape(total, META).astype(F32).T
    glane = lax.broadcasted_iota(jnp.int32, (8, total), 1)
    gslot = lax.rem(glane, BLK)
    count_l = jnp.broadcast_to(lanes[1:2], (8, total))
    first = jnp.where(gslot == 0, count_l, 0.0).astype(BF16)
    start_l = dot(first, held[0])
    wide = gslot.astype(F32)
    left = jnp.where(wide < count_l, start_l + wide, -1.0)[:1]
    wide = wide - CAP
    right = jnp.where((wide >= 0) & (wide < count_l), start_l + wide, -1.0)[:1]
    place = lax.broadcasted_iota(jnp.int32, (rows, total), 0).astype(F32)
    left = jnp.where(left == place, 1.0, 0.0).astype(BF16)
    right = jnp.where(right == place, 1.0, 0.0).astype(BF16)

    square = jnp.zeros((rows, 1), F32)
    for h, pick in enumerate((left, right)):
        for j in range(nch):
            cut = slice(j * CHUNK, (j + 1) * CHUNK)
            got = dot(pick, grid[:, :, :, :, cut].reshape(total, CHUNK))
            square = square + jnp.sum(got * got, axis=1, keepdims=True)
            picked[h, :, cut] = got.astype(BF16)
    scale = lax.rsqrt(square / d + 1e-05)
    for h in range(2):
        for j in range(nch):
            cut = slice(j * CHUNK, (j + 1) * CHUNK)
            normed[h, :, cut] = (
                picked[h, :, cut].astype(F32) * scale * again_ref[h, :, cut]).astype(BF16)

    get_wkv.wait()
    kvp[...] = dot(normed[f], wkv[...])
    kvp_in_copy = remote(kvp, kvp_in, sib)
    info = dot(left, grid[:, :, :, :, half:].reshape(total, META))
    position = info[:, 2:3] * tok_rows + info[:, 0:1]
    lane = lax.broadcasted_iota(jnp.int32, (rows, 128), 1)
    freq = jnp.exp(-math.log(500000.0) * lax.rem(lane, 64).astype(F32) * 2.0 / 128)
    angle = position * freq
    cosine = jnp.cos(angle)
    sine = jnp.where(lane < 64, -1.0, 1.0) * jnp.sin(angle)
    get_wq.wait()
    query = rope(dot(normed[0], wq[:half]) + dot(normed[1], wq[half:]), cosine, sine).astype(BF16)
    kvp_in_copy.wait_recv()
    both = kvp[...] + kvp_in[...]
    holds_keys = lo == 0
    kv[...] = jnp.where(holds_keys, rope(both, cosine, sine), both).astype(BF16)
    kv_copy = remote(kv, kv_in, pair)
    kv_copy.wait_recv()
    keys = jnp.where(holds_keys, kv[...].astype(F32), kv_in[...].astype(F32)).astype(BF16)
    values = jnp.where(holds_keys, kv_in[...].astype(F32), kv[...].astype(F32)).astype(BF16)
    scores = lax.dot_general(query, keys, (((1,), (1,)), ((), ())), preferred_element_type=F32)
    scores = scores * (1.0 / math.sqrt(128))
    seen = lax.broadcasted_iota(jnp.int32, (rows, rows), 1) <= lax.broadcasted_iota(
        jnp.int32, (rows, rows), 0)
    scores = jnp.where(seen, scores, -1e30)
    weights = jnp.exp(scores - jnp.max(scores, axis=1, keepdims=True))
    probs = (weights / jnp.sum(weights, axis=1, keepdims=True)).astype(BF16)
    mix[f] = dot(probs, values).astype(BF16)
    mix_copy = remote(mix.at[f], mix.at[f], sib)
    get_wo.wait()
    wo_in.wait_recv()
    mix_copy.wait_recv()

    def scatter(part, order, size, pbuf, rbuf, sbuf, tbuf, take):
        passed = []
        for j in range(half // SUM):
            value = part(j)
            for a in range(2):
                for b in range(m):
                    at = order(a, b) * size
                    pbuf[j, a, b] = value[at:at + size].astype(BF16)
            passed.append(remote(pbuf.at[j, 1 - lo], rbuf.at[j], pair))
        spread = []
        for j in range(half // SUM):
            passed[j].wait_recv()
            sbuf[j] = (pbuf[j, lo].astype(F32) + rbuf[j].astype(F32)).astype(BF16)
            spread.append([
                remote(sbuf.at[j, lax.rem(hi + k, m)], tbuf.at[j, k - 1], across(k))
                for k in range(1, m)])
        for j in range(half // SUM):
            whole = pbuf[j, lo, hi].astype(F32) + rbuf[j, hi].astype(F32)
            for k in range(1, m):
                spread[j][k - 1].wait_recv()
                whole = whole + tbuf[j, k - 1].astype(F32)
            take(j, whole)

    mixed = jnp.concatenate([mix[0], mix[1]], axis=1)

    def project(j):
        cut = slice(j * SUM, (j + 1) * SUM)
        return dot(mixed, wo[:, :, cut].reshape(256, SUM))

    own = pl.ds(pl.multiple_of(c * ROW, ROW), ROW)

    def keep(j, whole):
        att[:, j * SUM:(j + 1) * SUM] = whole

    scatter(project, lambda a, b: b * 2 + a, ROW, pb, rb, sb, tb, keep)

    resid = picked[f, own, :].astype(F32) + att[...]
    ssq[0] = jnp.broadcast_to(jnp.sum(resid * resid, axis=1, keepdims=True), (ROW, 128))
    remote(ssq.at[0], ssq.at[1], sib).wait_recv()
    scale2 = lax.rsqrt((ssq[0] + ssq[1])[:, :1] / d + 1e-05)
    n2[lo, hi] = (resid * scale2 * fgain_ref[f]).astype(BF16)
    def expansion():
        sub = lax.broadcasted_iota(jnp.int32, (slots, META), 0)
        count_s = meta[:, 1:2]
        lead = jnp.where(lax.rem(sub, CAP) == 0, meta[...], 0.0).astype(BF16)
        tri_s = shard_of(lax.broadcasted_iota(jnp.int32, (1, slots), 1) // CAP) < shard_of(
            lax.broadcasted_iota(jnp.int32, (slots, 1), 0) // CAP)
        start_s = dot(tri_s.astype(F32).astype(BF16), lead)[:, 1:2]
        slot_s = lax.rem(sub, CAP)[:, :1].astype(F32)
        target = jnp.where(slot_s < count_s, start_s + slot_s, -1.0)
        p = lax.broadcasted_iota(jnp.int32, (1, rows), 1)
        natural = (lax.rem(p // ROW, m) * 2 + p // (ROW * m)) * ROW + lax.rem(p, ROW)
        held.append(jnp.where(target == natural.astype(F32), 1.0, 0.0).astype(BF16))

    gather(n2.at[lo, hi], lambda a, b: n2.at[a, b], half, False, expansion)
    expand = held[1]

    get_wg.wait()
    get_wu.wait()
    ff = wg.shape[1]
    hrows = rows // 2
    away = n2[1 - f].reshape(hrows, half)
    gu[0] = dot(away, wg[...]).astype(BF16)
    gu[1] = dot(away, wu[...]).astype(BF16)
    gu_copy = remote(gu, gu_in, sib)
    home = n2[f].reshape(hrows, half)
    gate = dot(home, wg[...])
    up = dot(home, wu[...])
    gu_copy.wait_recv()
    gate = gate + gu_in[0].astype(F32)
    up = up + gu_in[1].astype(F32)
    hid[f] = (gate / (1.0 + jnp.exp(-gate)) * up).astype(BF16)
    hid_copy = remote(hid.at[f], hid.at[f], sib)

    get_wd.wait()
    hid_copy.wait_recv()
    hidden = hid[...].reshape(rows, ff)
    own_perm = pl.ds(pl.multiple_of((lo * m + hi) * ROW, ROW), ROW)

    def feed(j):
        cut = slice(j * SUM, (j + 1) * SUM)
        pc[...] = dot(hidden, wd[:, cut])
        pc[own_perm, :] += att[:, cut]
        return dot(expand, pc[...].astype(BF16))

    def deliver(j, whole):
        cut = slice(j * SUM, (j + 1) * SUM)
        dl[0, :, cut] = whole[:CAP]
        dl[1, :, cut] = whole[CAP:]

    scatter(feed, lambda a, b: a * m + b, BLK, pd, rd, sd, td, deliver)
    remote(dl.at[1 - f], dr, sib).wait_recv()
    out_ref[f] = dl[f]
    out_ref[1 - f] = dr[...]
    for copy in sent:
        copy.wait_send()


def body(
    tokens, routed_index, routed_count, router_weight, attn_gain, ffn_gain,
    w_query, w_keyvalue, w_out, w_gate, w_up, w_down,
):
    tok_rows, d = tokens.shape
    half = d // 2
    n = lax.axis_size("ctx")
    m = n // 2
    shards = 2 * n
    rows = 16 * shards
    slots = shards * CAP
    nch = half // SUM
    ff = w_gate.shape[1]
    index_row = routed_index[0]
    picked = jnp.take(tokens, index_row, axis=0)
    shard = lax.axis_index("ctx") * 2 + lax.axis_index("fsdp")
    lane = jnp.arange(META)[None, :]
    facts = jnp.where(
        lane == 0, index_row[:, None],
        jnp.where(lane == 1, routed_count[0], jnp.where(lane == 2, shard, 0))).astype(BF16)
    block = jnp.concatenate(
        [jnp.concatenate([picked[:, :half], facts], 1),
         jnp.concatenate([picked[:, half:], facts], 1)], 0)
    copies = PIECES * (6 * m) + 2 * nch * m + 8
    vm = pl.BlockSpec(memory_space=pltpu.VMEM)
    hbm = pl.BlockSpec(memory_space=pl.ANY)
    flops = 2 * rows * half * ff * 3
    delta = pl.pallas_call(
        functools.partial(kernel, m, d, tok_rows),
        out_shape=jax.ShapeDtypeStruct((2, CAP, half), F32),
        in_specs=[vm] * 3 + [hbm] * 6,
        out_specs=vm,
        scratch_shapes=[
            pltpu.VMEM((2, m, 2, BLK, half + META), BF16),
            pltpu.VMEM(w_query.shape, BF16),
            pltpu.VMEM(w_keyvalue.shape, BF16),
            pltpu.VMEM((2, 128, half), BF16),
            pltpu.VMEM(w_gate.shape, BF16),
            pltpu.VMEM(w_up.shape, BF16),
            pltpu.VMEM(w_down.shape, BF16),
            pltpu.VMEM((slots, META), F32),
            pltpu.VMEM((2, rows, half), BF16),
            pltpu.VMEM((2, rows, half), BF16),
            pltpu.VMEM((rows, 128), F32),
            pltpu.VMEM((rows, 128), F32),
            pltpu.VMEM((rows, 128), BF16),
            pltpu.VMEM((rows, 128), BF16),
            pltpu.VMEM((2, rows, 128), BF16),
            pltpu.VMEM((nch, 2, m, ROW, SUM), BF16),
            pltpu.VMEM((nch, m, ROW, SUM), BF16),
            pltpu.VMEM((nch, m, ROW, SUM), BF16),
            pltpu.VMEM((nch, m - 1, ROW, SUM), BF16),
            pltpu.VMEM((ROW, half), F32),
            pltpu.VMEM((2, ROW, 128), F32),
            pltpu.VMEM((2, m, ROW, half), BF16),
            pltpu.VMEM((2, rows // 2, ff), BF16),
            pltpu.VMEM((2, rows // 2, ff), BF16),
            pltpu.VMEM((2, rows // 2, ff), BF16),
            pltpu.VMEM((rows, SUM), F32),
            pltpu.VMEM((nch, 2, m, BLK, SUM), BF16),
            pltpu.VMEM((nch, m, BLK, SUM), BF16),
            pltpu.VMEM((nch, m, BLK, SUM), BF16),
            pltpu.VMEM((nch, m - 1, BLK, SUM), BF16),
            pltpu.VMEM((2, CAP, half), F32),
            pltpu.VMEM((CAP, half), F32),
            pltpu.SemaphoreType.DMA((6,)),
            pltpu.SemaphoreType.DMA((copies,)),
            pltpu.SemaphoreType.DMA((copies,)),
        ],
        compiler_params=pltpu.CompilerParams(
            collective_id=0, has_side_effects=True, vmem_limit_bytes=60 * 1024 * 1024),
        cost_estimate=pl.CostEstimate(flops=flops, bytes_accessed=14 << 20, transcendentals=0),
        name="depth_block",
    )(block, attn_gain.reshape(2, 1, half), ffn_gain.reshape(2, 1, half),
      w_query, w_keyvalue, w_out, w_gate, w_up, w_down)
    base = picked.astype(F32)
    router = jax.nn.sigmoid(jnp.dot(base, router_weight, precision=lax.Precision.HIGHEST))
    delta = jnp.concatenate([delta[0], delta[1]], axis=1)
    updated = (base + router[:, None] * delta).astype(BF16)
    live = jnp.arange(CAP, dtype=jnp.int32) < routed_count[0]
    hit = (jnp.arange(tok_rows, dtype=jnp.int32)[:, None] == index_row[None, :]) & live[None, :]
    placed = jnp.dot(hit.astype(BF16), updated, preferred_element_type=F32).astype(BF16)
    return jnp.where(jnp.any(hit, axis=1)[:, None], placed, tokens)


def solution(mesh):
    placed = (
        P(("groups", "ctx", "fsdp"), None),
        P(("groups", "ctx", "fsdp"), None),
        P(("groups", "ctx", "fsdp")),
        P(),
        P(),
        P(),
        P(None, ("ctx", "fsdp")),
        P("fsdp", "ctx"),
        P(("ctx", "fsdp"), None),
        P("fsdp", "ctx"),
        P("fsdp", "ctx"),
        P("ctx", "fsdp"),
    )
    return jax.shard_map(
        body,
        mesh=mesh,
        in_specs=placed,
        out_specs=P(("groups", "ctx", "fsdp"), None),
        check_vma=False,
    )
```
